256 devices in a mesh: section: 32 (over y, z), tensor: 8 (over x, core).
Axes of the slice: x: 4, y: 4, z: 8, core: 2. Of those that a mesh axis runs over, the one named last changes fastest.
Arguments:
- pending_activations: bfloat16 [4096, 4096], P('section', 'tensor'), may hold values from -6 to 6
- embedded_segments: bfloat16 [256, 4096], P(None, 'tensor'), may hold values from -6 to 6
- asking_mapping_matrix: bfloat16 [32, 4096, 4096], P('section', None, 'tensor'), may hold values from -0.09375 to 0.09375
- pair_mapping_matrix: bfloat16 [32, 4096, 2048], P('section', None, 'tensor'), may hold values from -0.09375 to 0.09375
- attention_exit_matrix: bfloat16 [32, 4096, 4096], P('section', 'tensor'), may hold values from -0.375 to 0.375
- memo_pair_table: bfloat16 [32, 3968, 2048], P('section', None, 'tensor'), may hold values from -3.5 to 3.5
- entry_rmsnorm_scale: float32 [32, 4096], P('section'), may hold values from 0.5 to 1.5
- asking_rmsnorm_scale: float32 [32, 128], P('section'), may hold values from 0.5 to 1.5
- lookup_rmsnorm_scale: float32 [32, 128], P('section'), may hold values from 0.5 to 1.5
- deepstack_visual_features: bfloat16 [384, 3, 4096], P('section', None, 'tensor'), may hold values from -6 to 6
- visual_feature_positions: int32 [384], P('section'), may hold values from 0 to 511, as said below
Outputs:
- hidden_out: bfloat16 [4096, 4096], P('section', 'tensor')
- kv_appended: bfloat16 [32, 256, 2048], P('section', None, 'tensor')
The draws below stay inside these ranges and needn't reach their ends.
Inputs may be any that keep to these rules, and one draw needn't show every extreme that they name: `visual_feature_positions`: distinct positions of the window of 512 rows that layers below 3 receive.
All inputs are finite; a program needn't handle non-finite values.
Results may differ from the reference program's by a relative error of at most 0.025.
Values may be sent and summed in bfloat16 or wider, within the bound.
A program may use at most 128 MiB of HBM per device.

```python
import jax
import jax.numpy as jnp
from jax import lax

EMBED_DIMENSION = 4096
QH = 32
KVH = 8
HD = 128
SEGMENT_SPAN = 128
STEPS = 2
LEVELS = 3
STACK_DEPTH = 32
CAP = 3968
ROWS = 384
N_SECTION = 32


def draw_visual_feature_positions(key, part):
    key = jax.random.fold_in(key, 11)
    span = (STEPS + LEVELS - 1) * SEGMENT_SPAN
    block_key, place_key, order_key = jax.random.split(key, 3)
    block_weight = jax.random.randint(block_key, (STEPS + LEVELS - 1,), 0, 6)
    noise = jax.random.randint(place_key, (span,), 0, 8)
    index = jnp.arange(span, dtype=jnp.int32)
    level = noise + block_weight[index // SEGMENT_SPAN]
    ends = (index == 0) | (index == span - 1)
    level = jnp.where(ends, -1, level)
    score = level * span + index
    chosen = jnp.argsort(score, stable=True)[:ROWS]
    order = jax.random.permutation(order_key, ROWS)
    return chosen[order].astype(jnp.int32)


def draw_memo_pair_table(key, part):
    key = jax.random.fold_in(key, 23)
    key_part, value_part = jax.random.split(key)
    array_extent = (STACK_DEPTH, CAP, KVH, 1, HD)
    key_entries = jax.random.uniform(key_part, array_extent, jnp.float32, -3.5, 3.5)
    value_entries = jnp.clip(jax.random.normal(value_part, array_extent, jnp.float32), -3.5, 3.5)
    joined = jnp.concatenate([key_entries, value_entries], axis=3)
    return joined.reshape(STACK_DEPTH, CAP, KVH * 2 * HD).astype(jnp.bfloat16)


def levels(own_key, extent, shards, smallest, high):
    def one(axis_at, blocks):
        steps = jax.random.uniform(jax.random.fold_in(jax.random.fold_in(own_key, 6), axis_at), (blocks,), jnp.float32, smallest / len(shards), high / len(shards))
        return jnp.repeat(jnp.exp(steps), extent[axis_at] // blocks).reshape((-1,) + (1,) * (len(extent) - axis_at - 1))

    level = one(*shards[0])
    for cut in shards[1:]:
        level = level * one(*cut)
    return level


def bell_draw(stream_key, shape, spread, bound, cuts=(), held_as=jnp.bfloat16):
    entries = jax.random.normal(stream_key, shape, jnp.float32) * spread
    if len(cuts) > 0:
        entries = levels(stream_key, shape, cuts, -0.22, 0.18) * entries
    return jnp.clip(entries, min=-bound, max=bound).astype(held_as)


def setup_inputs(seed: int = 0) -> dict:
    seeds = jax.random.split(jax.random.key(seed), 12)
    return {
        "pending_activations": bell_draw(seeds[0], (STACK_DEPTH * SEGMENT_SPAN, EMBED_DIMENSION), 1.0, 6.0, ((0, 32), (1, 8))),
        "embedded_segments": bell_draw(seeds[1], (STEPS * SEGMENT_SPAN, EMBED_DIMENSION), 1.0, 6.0, ((1, 8),)),
        "asking_mapping_matrix": bell_draw(seeds[2], (STACK_DEPTH, EMBED_DIMENSION, QH * HD), EMBED_DIMENSION ** -0.5, 0.09375, ((0, 32), (2, 8))),
        "pair_mapping_matrix": bell_draw(seeds[3], (STACK_DEPTH, EMBED_DIMENSION, KVH * 2 * HD), EMBED_DIMENSION ** -0.5, 0.09375, ((0, 32), (2, 8))),
        "attention_exit_matrix": bell_draw(seeds[4], (STACK_DEPTH, QH * HD, EMBED_DIMENSION), (QH * HD // 16) ** -0.5, 0.375, ((0, 32), (1, 8))),
        "memo_pair_table": draw_memo_pair_table(jax.random.fold_in(seeds[11], 71), 0),
        "entry_rmsnorm_scale": jnp.clip(1.0 + 0.1 * jax.random.normal(seeds[6], (STACK_DEPTH, EMBED_DIMENSION), jnp.float32), 0.5, 1.5),
        "asking_rmsnorm_scale": jnp.clip(1.0 + 0.1 * jax.random.normal(seeds[7], (STACK_DEPTH, HD), jnp.float32), 0.5, 1.5),
        "lookup_rmsnorm_scale": jnp.clip(1.0 + 0.1 * jax.random.normal(seeds[8], (STACK_DEPTH, HD), jnp.float32), 0.5, 1.5),
        "deepstack_visual_features": bell_draw(seeds[9], (ROWS, LEVELS, EMBED_DIMENSION), 1.0, 6.0, ((0, 32), (2, 8))),
        "visual_feature_positions": draw_visual_feature_positions(jax.random.fold_in(seeds[11], 71), 0),
    }


epsilon = 1e-06
rope_theta = 5000000.0

def rotary(values, position):
    head_width = values.shape[-1]
    half_width = head_width // 2
    frequency = rope_theta ** (-(jnp.arange(half_width, dtype=jnp.float32) * 2.0 / head_width))
    angles = position.astype(jnp.float32)[:, None] * frequency[None, :]
    cos_part = jnp.cos(angles)[:, None, :]
    sin_part = jnp.sin(angles)[:, None, :]
    lower_half = values[..., :half_width]
    upper_half = values[..., half_width:]
    return jnp.concatenate([lower_half * cos_part - upper_half * sin_part, upper_half * cos_part + lower_half * sin_part], axis=-1)

def rms_scale(values, gain):
    return values * lax.rsqrt(lax.optimization_barrier(jnp.mean(values * values, axis=-1, keepdims=True)) + epsilon) * gain

def attention(query, keys, values, valid):
    scores = jnp.einsum('ckgh,pkh->kgcp', query.astype(jnp.float32), keys.astype(jnp.float32)) * query.shape[-1] ** (-0.5)
    weights = jnp.where(valid[None, None], jnp.exp(scores), 0.0)
    total = lax.optimization_barrier(jnp.sum(weights, axis=-1))
    rounded = weights.astype(jnp.bfloat16)
    summed = jnp.einsum('kgcp,pkh->ckgh', rounded.astype(jnp.float32), values.astype(jnp.float32))
    return (summed / jnp.transpose(total, (2, 0, 1))[..., None]).astype(jnp.bfloat16)

def layer(section_id, step_no, rows, query_w, keyval_w, out_w, cached, in_gain, q_gain, k_gain, appended, deepstack_visual_features, visual_feature_positions):
    rows_f = rows.astype(jnp.float32)
    normed = rms_scale(rows_f, in_gain).astype(jnp.bfloat16)
    query = jnp.dot(normed, query_w, preferred_element_type=jnp.float32)
    keyval = jnp.dot(normed, keyval_w, preferred_element_type=jnp.float32).reshape(SEGMENT_SPAN, KVH, 2, HD)
    offset = (N_SECTION - 1 - section_id) * SEGMENT_SPAN
    position = offset + step_no * SEGMENT_SPAN + jnp.arange(SEGMENT_SPAN, dtype=jnp.int32)
    query = rotary(rms_scale(query.reshape(SEGMENT_SPAN, QH, HD), q_gain), position)
    query = query.astype(jnp.bfloat16).reshape(SEGMENT_SPAN, KVH, QH // KVH, HD)
    keys_new = rotary(rms_scale(keyval[:, :, 0], k_gain), position)
    fresh = jnp.stack([keys_new, keyval[:, :, 1]], axis=2).astype(jnp.bfloat16)
    appended = appended.at[step_no * SEGMENT_SPAN:(step_no + 1) * SEGMENT_SPAN].set(fresh)
    all_keys = jnp.concatenate([cached[:, :, 0], appended[:, :, 0]], axis=0)
    all_values = jnp.concatenate([cached[:, :, 1], appended[:, :, 1]], axis=0)
    cache_valid = jnp.broadcast_to(jnp.arange(CAP, dtype=jnp.int32)[None, :] < offset, (SEGMENT_SPAN, CAP))
    fresh_valid = jnp.arange(STEPS * SEGMENT_SPAN, dtype=jnp.int32)[None, :] <= step_no * SEGMENT_SPAN + jnp.arange(SEGMENT_SPAN, dtype=jnp.int32)[:, None]
    valid = jnp.concatenate([cache_valid, fresh_valid], axis=1)
    attended = attention(query, all_keys, all_values, valid).reshape(SEGMENT_SPAN, QH * HD)
    mixed = jnp.dot(attended, out_w, preferred_element_type=jnp.float32)
    level = jnp.minimum(section_id, LEVELS - 1)
    chosen = lax.dynamic_index_in_dim(deepstack_visual_features, level, 1, keepdims=False)
    window = step_no + LEVELS - 1 - section_id
    targets = window * SEGMENT_SPAN + jnp.arange(SEGMENT_SPAN, dtype=jnp.int32)
    onehot = ((visual_feature_positions[None, :] == targets[:, None]) & (section_id < LEVELS)).astype(jnp.bfloat16)
    injected = jnp.dot(onehot, chosen, preferred_element_type=jnp.float32)
    return ((rows_f + mixed + injected).astype(jnp.bfloat16), appended)

def reference(pending_activations, embedded_segments, asking_mapping_matrix, pair_mapping_matrix, attention_exit_matrix, memo_pair_table, entry_rmsnorm_scale, asking_rmsnorm_scale, lookup_rmsnorm_scale, deepstack_visual_features, visual_feature_positions):
    layer_ids = jnp.arange(STACK_DEPTH, dtype=jnp.int32)
    result_lines = pending_activations.reshape(STACK_DEPTH, SEGMENT_SPAN, EMBED_DIMENSION)
    cached = memo_pair_table.reshape(STACK_DEPTH, CAP, KVH, 2, HD)
    appended = jnp.zeros((STACK_DEPTH, STEPS * SEGMENT_SPAN, KVH, 2, HD), jnp.bfloat16)
    for step_no in range(STEPS):
        entering = embedded_segments[step_no * SEGMENT_SPAN:(step_no + 1) * SEGMENT_SPAN][None]
        inputs = jnp.concatenate([entering, result_lines[:-1]], axis=0)

        def one_layer(pack):
            return layer(pack[0], step_no, pack[1], pack[2], pack[3], pack[4], pack[5], pack[6], pack[7], pack[8], pack[9], deepstack_visual_features, visual_feature_positions)
        result_lines, appended = lax.map(one_layer, (layer_ids, inputs, asking_mapping_matrix, pair_mapping_matrix, attention_exit_matrix, cached, entry_rmsnorm_scale, asking_rmsnorm_scale, lookup_rmsnorm_scale, appended))
    return (result_lines.reshape(STACK_DEPTH * SEGMENT_SPAN, EMBED_DIMENSION), appended.reshape(STACK_DEPTH, STEPS * SEGMENT_SPAN, KVH * 2 * HD))
```

```python
import functools
import math

import jax
import jax.numpy as jnp
from jax import lax
from jax.experimental import pallas as pl
from jax.experimental.pallas import tpu as pltpu
from jax.sharding import PartitionSpec as P

MESH = pl.DeviceIdType.MESH
EPS = 1e-06
THETA = 5000000.0
PAD = 16
F32 = jnp.float32
BF16 = jnp.bfloat16


def kernel(
    sections,
    pend,
    emb,
    wq_h,
    wkv_h,
    wo_h,
    memo,
    in_gain_h,
    q_gain_h,
    k_gain_h,
    feat_h,
    pos,
    out,
    kv_out,
    wqkv,
    wo,
    kv,
    in_gain,
    q_gain,
    k_gain,
    feat,
    msg,
    fbuf,
    inj,
    cs,
    sn,
    xb,
    ss,
    acc,
    qs,
    pv,
    att,
    sib_src,
    sib_dst,
    opp_src,
    rel_dst,
    nb_src,
    nb_dst,
    keep,
    yb,
    load_sem,
    emb_sem,
    fs_sem,
    fr_sem,
    ags,
    agr,
    rss,
    rsr,
    out_sem,
):
    S = sections
    steps, T, R, C = xb.shape
    half = R // 2
    HD = 128
    HC = att.shape[1]
    G = HC // HD
    D = T * C
    rows, levels = feat.shape[0], feat.shape[1]
    chunk = 4 * R
    s = lax.axis_index("section")
    me = lax.axis_index("tensor")
    x = me // 2
    c = me % 2
    ring = T // 2

    def block(step, parity):
        return 2 * ((x + step) % ring) + parity

    sib = block(0, 1 - c)
    right, left, opp = block(1, c), block(ring - 1, c), block(2, c)
    sright, sleft, sopp = block(1, 1 - c), block(ring - 1, 1 - c), block(2, 1 - c)
    off = pl.multiple_of((S - 1 - s) * R, R)

    ends = [
        (feat_h, feat),
        (in_gain_h, in_gain),
        (q_gain_h, q_gain),
        (k_gain_h, k_gain),
        (wq_h, wqkv.at[:, :, pl.ds(0, HC)]),
        (wkv_h, wqkv.at[:, :, pl.ds(HC, 2 * HD)]),
        (memo, kv.at[pl.ds(0, memo.shape[0])]),
    ] + [(wo_h.at[:, pl.ds(j * C, C)], wo.at[j]) for j in range(T)]

    def load(i):
        return pltpu.make_async_copy(*ends[i], load_sem.at[i])

    for i in range(7 + T):
        load(i).start()

    def enter(step):
        return pltpu.make_async_copy(
            emb.at[pl.ds(step * R, R)], xb.at[step, me], emb_sem.at[step]
        )

    @pl.when(s == 0)
    def _():
        for step in range(steps):
            enter(step).start()

    barrier = pltpu.get_barrier_semaphore()
    for peer in (sib, right, left):
        pl.semaphore_signal(barrier, inc=1, device_id={"tensor": peer}, device_id_type=MESH)

    @pl.when(s < levels)
    def _():
        def greet(k, carry):
            @pl.when(k != s)
            def _():
                pl.semaphore_signal(barrier, inc=1, device_id={"section": k}, device_id_type=MESH)

            return carry

        lax.fori_loop(0, S, greet, 0)

    @pl.when(s >= levels)
    def _():
        pl.semaphore_signal(barrier, inc=1, device_id={"section": s - 1}, device_id_type=MESH)

    peers = 3 + levels - jnp.where(s < levels, 1, 0)
    peers = peers + jnp.where((s >= levels - 1) & (s < S - 1), 1, 0)
    pl.semaphore_wait(barrier, peers)

    def shift(source, step, h):
        return pltpu.make_async_remote_copy(
            src_ref=source.at[pl.ds(h * half, half)],
            dst_ref=xb.at[step, me, pl.ds(h * half, half)],
            send_sem=ags.at[step, h],
            recv_sem=agr.at[step, h],
            device_id={"section": jnp.minimum(s + 1, S - 1)},
            device_id_type=MESH,
        )

    @pl.when(s < S - 1)
    def _():
        for h in range(2):
            shift(pend, 0, h).start()

    for i in range(4):
        load(i).wait()
    col = lax.broadcasted_iota(jnp.int32, (PAD, steps * R), 1)
    row = lax.broadcasted_iota(jnp.int32, (PAD, steps * R), 0)
    place = jnp.full((PAD, steps * R), -1000000, jnp.int32)
    for r in range(rows):
        place = jnp.where(row == r, pos[r], place)
    msg[...] = jnp.zeros_like(msg)
    everything = feat[...].astype(F32)
    for level in range(levels):
        msg[level, 0:rows, 0:C] = everything[:, level, :].astype(BF16)
        hit = place - (levels - 1 - level) * R == col
        msg[level, :, C:] = jnp.where(hit, 1.0, 0.0).astype(BF16)

    def feature(level):
        return pltpu.make_async_remote_copy(
            src_ref=msg.at[level],
            dst_ref=fbuf.at[pl.ds(s * PAD, PAD)],
            send_sem=fs_sem.at[level],
            recv_sem=fr_sem,
            device_id={"section": level},
            device_id_type=MESH,
        )

    for level in range(levels):

        @pl.when(s != level)
        def _():
            feature(level).start()

        @pl.when(s == level)
        def _():
            fbuf[pl.ds(pl.multiple_of(s * PAD, PAD), PAD), :] = msg[level]

    lane = lax.broadcasted_iota(jnp.int32, (R, HD), 1)
    fold = jnp.where(lane < HD // 2, lane, lane - HD // 2).astype(F32)
    frequency = jnp.exp(fold * (-2.0 * math.log(THETA) / HD))
    for step in range(steps):
        place = off + step * R + lax.broadcasted_iota(jnp.int32, (R, HD), 0)
        angle = place.astype(F32) * frequency
        cs[step] = jnp.cos(angle)
        sn[step] = jnp.where(lane < HD // 2, -jnp.sin(angle), jnp.sin(angle))
    tail = kv.shape[0] - memo.shape[0]
    kv[pl.ds(memo.shape[0], tail), :] = jnp.zeros((tail, 2 * HD), BF16)

    for i in (4, 5):
        load(i).wait()

    def step_body(t, carry):
        def piece(b, h):
            return xb.at[t, b, pl.ds(h * half, half)]

        def gather(slot_out, b, h, peer, slot_in):
            return pltpu.make_async_remote_copy(
                src_ref=piece(b, h),
                dst_ref=piece(b, h),
                send_sem=ags.at[t, slot_out],
                recv_sem=agr.at[t, slot_in],
                device_id={"tensor": peer},
                device_id_type=MESH,
            )

        sends = []

        def send(*args):
            copy = gather(len(sends) + 2, *args)
            copy.start()
            sends.append(copy)

        def arrived(slot, b, h):
            gather(0, b, h, sib, slot).wait_recv()

        def project(b):
            rows_f = xb[t, b].astype(F32)
            square = rows_f * rows_f
            total = square[:, 0:HD]
            for g in range(1, C // HD):
                total = total + square[:, g * HD : (g + 1) * HD]
            ss[...] += total
            gain = in_gain[:, pl.ds(pl.multiple_of(b * C, C), C)]
            acc[...] += jnp.dot(
                (rows_f * gain).astype(BF16), wqkv[b], preferred_element_type=F32
            )

        ss[...] = jnp.zeros_like(ss)
        acc[...] = jnp.zeros_like(acc)

        @pl.when(s == 0)
        def _():
            enter(t).wait()

        for h in range(2):

            @pl.when(s > 0)
            def _():
                arrived(h, me, h)

            send(me, h, right, 4 + h)
            send(me, h, left, 6 + h)
            send(me, h, sib, 2 + h)
        project(me)
        arrived(4, left, 0)
        send(left, 0, right, 12)
        send(left, 0, sib, 8)
        arrived(7, right, 1)
        send(right, 1, left, 13)
        send(right, 1, sib, 11)
        arrived(5, left, 1)
        send(left, 1, sib, 9)
        arrived(6, right, 0)
        send(right, 0, sib, 10)
        arrived(2, sib, 0)
        arrived(3, sib, 1)
        project(sib)
        project(left)
        project(right)
        arrived(12, opp, 0)
        send(opp, 0, sib, 14)
        arrived(13, opp, 1)
        send(opp, 1, sib, 15)
        project(opp)
        arrived(8, sleft, 0)
        arrived(9, sleft, 1)
        project(sleft)
        arrived(10, sright, 0)
        arrived(11, sright, 1)
        project(sright)
        arrived(14, sopp, 0)
        arrived(15, sopp, 1)
        project(sopp)

        scale = lax.rsqrt(jnp.sum(ss[...], axis=-1, keepdims=True) * (1.0 / D) + EPS)
        cos, sin = cs[t], sn[t]

        def head(value, gain):
            value = value * scale
            mean = jnp.sum(value * value, axis=-1, keepdims=True) * (1.0 / HD)
            value = value * lax.rsqrt(mean + EPS) * gain
            return value * cos + pltpu.roll(value, HD // 2, 1) * sin

        for g in range(G):
            query = head(acc[:, g * HD : (g + 1) * HD], q_gain[...])
            qs[g * R : (g + 1) * R, :] = (query * (math.log2(math.e) * HD**-0.5)).astype(BF16)

        @pl.when(t == 0)
        def _():
            load(6).wait()

        here = pl.ds(pl.multiple_of(off + t * R, R), R)
        kv[here, 0:HD] = head(acc[:, HC : HC + HD], k_gain[...]).astype(BF16)
        kv[here, HD:] = (acc[:, HC + HD :] * scale).astype(BF16)
        appended(t).start()

        pv[...] = jnp.zeros_like(pv)
        first = off + t * R
        whole = first // chunk

        def attend(at, masked):
            keys = kv[pl.ds(pl.multiple_of(at * chunk, chunk), chunk), :]
            values = jnp.concatenate([keys[:, HD:], jnp.ones((chunk, HD), BF16)], axis=1)
            for g in range(G):
                score = lax.dot_general(
                    qs[g * R : (g + 1) * R, :],
                    keys[:, 0:HD],
                    (((1,), (1,)), ((), ())),
                    preferred_element_type=F32,
                )
                weight = jnp.exp2(score)
                if masked:
                    slot = at * chunk + lax.broadcasted_iota(jnp.int32, (R, chunk), 1)
                    last = first + lax.broadcasted_iota(jnp.int32, (R, chunk), 0)
                    weight = jnp.where(slot <= last, weight, 0.0)
                pv[g * R : (g + 1) * R, :] += jnp.dot(
                    weight.astype(BF16), values, preferred_element_type=F32
                )

        def whole_chunk(at, carry):
            attend(at, False)
            return carry

        lax.fori_loop(0, whole, whole_chunk, 0)
        attend(whole, True)
        for g in range(G):
            found = pv[g * R : (g + 1) * R, :]
            att[:, g * HD : (g + 1) * HD] = (found[:, 0:HD] / found[:, HD:]).astype(BF16)

        @pl.when(t == 0)
        def _():
            for j in range(T):
                load(7 + j).wait()

        def part(b):
            return jnp.dot(att[...], wo[b], preferred_element_type=F32)

        def reduce(slot, source, target, peer):
            return pltpu.make_async_remote_copy(
                src_ref=source,
                dst_ref=target,
                send_sem=rss.at[t, slot],
                recv_sem=rsr.at[t, slot],
                device_id={"tensor": peer},
                device_id_type=MESH,
            )

        top, low = pl.ds(0, half), pl.ds(half, half)
        moves = [
            reduce(d, sib_src.at[t, d], sib_dst.at[t, d], sib) for d in range(4)
        ] + [
            reduce(4, opp_src.at[t, top], rel_dst.at[t, 0], right),
            reduce(5, opp_src.at[t, low], rel_dst.at[t, 1], left),
            reduce(6, nb_src.at[t, 0, low], nb_dst.at[t, 0, low], right),
            reduce(7, nb_src.at[t, 1, top], nb_dst.at[t, 1, top], left),
            reduce(8, nb_src.at[t, 0, top], nb_dst.at[t, 0, top], right),
            reduce(9, nb_src.at[t, 1, low], nb_dst.at[t, 1, low], left),
        ]
        for d, b in enumerate((sopp, sright, sleft)):
            sib_src[t, d] = part(b).astype(BF16)
            moves[d].start()
        value = part(opp)
        moves[0].wait_recv()
        opp_src[t] = (value + sib_dst[t, 0].astype(F32)).astype(BF16)
        moves[4].start()
        moves[5].start()
        value = part(right)
        moves[1].wait_recv()
        value = value + sib_dst[t, 1].astype(F32)
        nb_src[t, 0, half:, :] = value[half:].astype(BF16)
        moves[6].start()
        keep[0] = value[0:half]
        value = part(left)
        moves[2].wait_recv()
        value = value + sib_dst[t, 2].astype(F32)
        nb_src[t, 1, 0:half, :] = value[0:half].astype(BF16)
        moves[7].start()
        keep[1] = value[half:]
        sib_src[t, 3] = part(sib).astype(BF16)
        moves[3].start()
        moves[4].wait_recv()
        nb_src[t, 0, 0:half, :] = (keep[0] + rel_dst[t, 0].astype(F32)).astype(BF16)
        moves[8].start()
        moves[5].wait_recv()
        nb_src[t, 1, half:, :] = (keep[1] + rel_dst[t, 1].astype(F32)).astype(BF16)
        moves[9].start()
        value = part(me) + xb[t, me].astype(F32)
        keep[0] = value[0:half]
        keep[1] = value[half:]

        @pl.when((t == 0) & (s < levels))
        def _():
            pltpu.make_async_remote_copy(
                src_ref=fbuf.at[pl.ds(0, (S - 1) * PAD)],
                dst_ref=fbuf.at[pl.ds(0, (S - 1) * PAD)],
                send_sem=fs_sem.at[0],
                recv_sem=fr_sem,
                device_id={"section": 0},
                device_id_type=MESH,
            ).wait_recv()
            for step in range(steps):
                inj[step] = lax.dot_general(
                    fbuf[:, C + step * R : C + (step + 1) * R],
                    fbuf[:, 0:C],
                    (((0,), (0,)), ((), ())),
                    preferred_element_type=F32,
                )

        @pl.when(s < levels)
        def _():
            keep[0] += inj[t, 0:half, :]
            keep[1] += inj[t, half:, :]

        moves[3].wait_recv()
        for h, (a, b) in enumerate(((8, 7), (6, 9))):
            moves[a].wait_recv()
            moves[b].wait_recv()
            these = slice(h * half, (h + 1) * half)
            yb[t, these, :] = (
                keep[h]
                + sib_dst[t, 3, these, :].astype(F32)
                + nb_dst[t, 0, these, :].astype(F32)
                + nb_dst[t, 1, these, :].astype(F32)
            ).astype(BF16)

            @pl.when((t == 0) & (s < S - 1))
            def _():
                shift(yb.at[0], 1, h).start()

        for copy in sends + moves:
            copy.wait_send()
        return carry

    def appended(step):
        return pltpu.make_async_copy(
            kv.at[pl.ds(pl.multiple_of(off + step * R, R), R)],
            kv_out.at[pl.ds(step * R, R)],
            out_sem.at[step],
        )

    lax.fori_loop(0, steps, step_body, 0)
    final = pltpu.make_async_copy(yb.at[steps - 1], out, out_sem.at[steps])
    final.start()
    for step in range(steps):
        appended(step).wait()

    @pl.when(s < S - 1)
    def _():
        for h in range(2):
            shift(pend, 0, h).wait_send()
            shift(yb.at[0], 1, h).wait_send()

    for level in range(levels):

        @pl.when(s != level)
        def _():
            feature(level).wait_send()

    final.wait()


def body(sections, tensors, pend, emb, wq, wkv, wo, memo, in_gain, q_gain, k_gain, feat, pos):
    R, C = pend.shape
    steps = emb.shape[0] // R
    D = C * tensors
    HC = wq.shape[2]
    HD = 128
    rows, levels = feat.shape[0], feat.shape[1]
    cap = memo.shape[1]
    chunk = 4 * R
    slots = -(-(cap + steps * R) // chunk) * chunk
    anyspec = pl.BlockSpec(memory_space=pl.ANY)
    V = pltpu.VMEM
    DMA = pltpu.SemaphoreType.DMA
    hidden, appended = pl.pallas_call(
        functools.partial(kernel, sections),
        out_shape=(
            jax.ShapeDtypeStruct((R, C), BF16),
            jax.ShapeDtypeStruct((steps * R, 2 * HD), BF16),
        ),
        in_specs=[anyspec] * 10 + [pl.BlockSpec(memory_space=pltpu.SMEM)],
        out_specs=(anyspec, anyspec),
        scratch_shapes=[
            V((tensors, C, HC + 2 * HD), BF16),
            V((tensors, HC, C), BF16),
            V((slots, 2 * HD), BF16),
            V((1, D), F32),
            V((1, HD), F32),
            V((1, HD), F32),
            V((rows, levels, C), BF16),
            V((levels, PAD, C + steps * R), BF16),
            V((sections * PAD, C + steps * R), BF16),
            V((steps, R, C), F32),
            V((steps, R, HD), F32),
            V((steps, R, HD), F32),
            V((steps, tensors, R, C), BF16),
            V((R, HD), F32),
            V((R, HC + 2 * HD), F32),
            V((HC // HD * R, HD), BF16),
            V((HC // HD * R, 2 * HD), F32),
            V((R, HC), BF16),
            V((steps, 4, R, C), BF16),
            V((steps, 4, R, C), BF16),
            V((steps, R, C), BF16),
            V((steps, 2, R // 2, C), BF16),
            V((steps, 2, R, C), BF16),
            V((steps, 2, R, C), BF16),
            V((2, R // 2, C), F32),
            V((steps, R, C), BF16),
            DMA((7 + tensors,)),
            DMA((steps,)),
            DMA((levels,)),
            DMA,
            DMA((steps, 16)),
            DMA((steps, 16)),
            DMA((steps, 10)),
            DMA((steps, 10)),
            DMA((steps + 1,)),
        ],
        compiler_params=pltpu.CompilerParams(
            collective_id=0, has_side_effects=True, vmem_limit_bytes=48 * 1024 * 1024
        ),
    )(
        pend,
        emb,
        wq.reshape(tensors, C, HC),
        wkv.reshape(tensors, C, 2 * HD),
        wo.reshape(HC, D),
        memo.reshape(cap, 2 * HD),
        in_gain,
        q_gain,
        k_gain,
        feat,
        pos,
    )
    return hidden, appended.reshape(1, steps * R, 2 * HD)


def solution(mesh):
    return jax.shard_map(
        functools.partial(body, mesh.shape["section"], mesh.shape["tensor"]),
        mesh=mesh,
        in_specs=(
            P("section", "tensor"),
            P(None, "tensor"),
            P("section", None, "tensor"),
            P("section", None, "tensor"),
            P("section", "tensor", None),
            P("section", None, "tensor"),
            P("section", None),
            P("section", None),
            P("section", None),
            P("section", None, "tensor"),
            P("section"),
        ),
        out_specs=(P("section", "tensor"), P("section", None, "tensor")),
        check_vma=False,
    )
```

```python
import functools
import math

import jax
import jax.numpy as jnp
from jax import lax
from jax.experimental import pallas as pl
from jax.experimental.pallas import tpu as pltpu
from jax.sharding import PartitionSpec as P

MESH = pl.DeviceIdType.MESH
EPS = 1e-06
THETA = 5000000.0
PAD = 16
F32 = jnp.float32
BF16 = jnp.bfloat16


def kernel(
    sections,
    pend,
    emb,
    wq_h,
    wkv_h,
    wo_h,
    memo,
    in_gain_h,
    q_gain_h,
    k_gain_h,
    feat_h,
    pos,
    out,
    kv_out,
    wqkv,
    wo,
    kv,
    in_gain,
    q_gain,
    k_gain,
    feat,
    msg,
    fbuf,
    inj,
    cs,
    sn,
    xb,
    ss,
    acc,
    qs,
    ps,
    pv,
    att,
    wo_sib,
    nb_src,
    nb_dst,
    keep,
    yb,
    load_sem,
    emb_sem,
    fs_sem,
    fr_sem,
    ags,
    agr,
    rss,
    rsr,
    ws,
    wr,
    out_sem,
):
    S = sections
    steps, T, R, C = xb.shape
    half = R // 2
    HD = 128
    HC = att.shape[3]
    G = HC // HD
    D = T * C
    rows, levels = feat.shape[0], feat.shape[1]
    chunk = 8 * R
    s = lax.axis_index("section")
    me = lax.axis_index("tensor")
    x = me // 2
    c = me % 2
    ring = T // 2

    def block(step, parity):
        return 2 * ((x + step) % ring) + parity

    sib = block(0, 1 - c)
    right, left, opp = block(1, c), block(ring - 1, c), block(2, c)
    sright, sleft, sopp = block(1, 1 - c), block(ring - 1, 1 - c), block(2, 1 - c)
    off = pl.multiple_of((S - 1 - s) * R, R)

    ends = [
        (feat_h, feat),
        (in_gain_h, in_gain),
        (q_gain_h, q_gain),
        (k_gain_h, k_gain),
        (wq_h, wqkv.at[:, :, pl.ds(0, HC)]),
        (wkv_h, wqkv.at[:, :, pl.ds(HC, 2 * HD)]),
        (memo, kv.at[pl.ds(0, memo.shape[0])]),
    ] + [
        (wo_h.at[:, pl.ds(pl.multiple_of((2 * j + c) * C, C), C)], wo.at[j])
        for j in range(ring)
    ]

    def load(i):
        return pltpu.make_async_copy(*ends[i], load_sem.at[i])

    for i in range(7 + ring):
        load(i).start()

    def enter(step):
        return pltpu.make_async_copy(
            emb.at[pl.ds(step * R, R)], xb.at[step, me], emb_sem.at[step]
        )

    @pl.when(s == 0)
    def _():
        for step in range(steps):
            enter(step).start()

    barrier = pltpu.get_barrier_semaphore()
    for peer in (sib, right, left, opp):
        pl.semaphore_signal(barrier, inc=1, device_id={"tensor": peer}, device_id_type=MESH)

    @pl.when(s < levels)
    def _():
        def greet(k, carry):
            @pl.when(k != s)
            def _():
                pl.semaphore_signal(barrier, inc=1, device_id={"section": k}, device_id_type=MESH)

            return carry

        lax.fori_loop(0, S, greet, 0)

    @pl.when(s >= levels)
    def _():
        pl.semaphore_signal(barrier, inc=1, device_id={"section": s - 1}, device_id_type=MESH)

    peers = 4 + levels - jnp.where(s < levels, 1, 0)
    peers = peers + jnp.where((s >= levels - 1) & (s < S - 1), 1, 0)
    pl.semaphore_wait(barrier, peers)

    def shift(source, step, h):
        return pltpu.make_async_remote_copy(
            src_ref=source.at[pl.ds(h * half, half)],
            dst_ref=xb.at[step, me, pl.ds(h * half, half)],
            send_sem=ags.at[step, h],
            recv_sem=agr.at[step, h],
            device_id={"section": jnp.minimum(s + 1, S - 1)},
            device_id_type=MESH,
        )

    @pl.when(s < S - 1)
    def _():
        for h in range(2):
            shift(pend, 0, h).start()

    def weights(j):
        return pltpu.make_async_remote_copy(
            src_ref=wo_h.at[:, pl.ds(pl.multiple_of((2 * j + 1 - c) * C, C), C)],
            dst_ref=wo_sib.at[j],
            send_sem=ws.at[j],
            recv_sem=wr.at[j],
            device_id={"tensor": sib},
            device_id_type=MESH,
        )

    for j in range(ring):
        weights(j).start()

    for i in range(4):
        load(i).wait()
    col = lax.broadcasted_iota(jnp.int32, (PAD, steps * R), 1)
    row = lax.broadcasted_iota(jnp.int32, (PAD, steps * R), 0)
    place = jnp.full((PAD, steps * R), -1000000, jnp.int32)
    for r in range(rows):
        place = jnp.where(row == r, pos[r], place)
    msg[...] = jnp.zeros_like(msg)
    everything = feat[...].astype(F32)
    for level in range(levels):
        msg[level, 0:rows, 0:C] = everything[:, level, :].astype(BF16)
        hit = place - (levels - 1 - level) * R == col
        msg[level, :, C:] = jnp.where(hit, 1.0, 0.0).astype(BF16)

    def feature(level):
        return pltpu.make_async_remote_copy(
            src_ref=msg.at[level],
            dst_ref=fbuf.at[pl.ds(s * PAD, PAD)],
            send_sem=fs_sem.at[level],
            recv_sem=fr_sem,
            device_id={"section": level},
            device_id_type=MESH,
        )

    for level in range(levels):

        @pl.when(s == level)
        def _():
            fbuf[pl.ds(pl.multiple_of(s * PAD, PAD), PAD), :] = msg[level]

    lane = lax.broadcasted_iota(jnp.int32, (R, HD), 1)
    fold = jnp.where(lane < HD // 2, lane, lane - HD // 2).astype(F32)
    frequency = jnp.exp(fold * (-2.0 * math.log(THETA) / HD))
    for step in range(steps):
        place = off + step * R + lax.broadcasted_iota(jnp.int32, (R, HD), 0)
        angle = place.astype(F32) * frequency
        cs[step] = jnp.cos(angle)
        sn[step] = jnp.where(lane < HD // 2, -jnp.sin(angle), jnp.sin(angle))
    tail = kv.shape[0] - memo.shape[0]
    kv[pl.ds(memo.shape[0], tail), :] = jnp.zeros((tail, 2 * HD), BF16)

    def piece(t, b, h):
        return xb.at[t, b, pl.ds(h * half, half)]

    def gather(t, h, k):
        b, peer, slot = (
            (me, opp, 12),
            (me, right, 4),
            (me, left, 6),
            (me, sib, 2),
            (left, sib, 8),
            (right, sib, 10),
            (opp, sib, 14),
        )[k]
        return pltpu.make_async_remote_copy(
            src_ref=piece(t, b, h),
            dst_ref=piece(t, b, h),
            send_sem=ags.at[t, 2 + 7 * h + k],
            recv_sem=agr.at[t, slot + h],
            device_id={"tensor": peer},
            device_id_type=MESH,
        )

    def arrived(t, h, slot, b):
        pltpu.make_async_remote_copy(
            src_ref=piece(t, b, h),
            dst_ref=piece(t, b, h),
            send_sem=ags.at[t, 2],
            recv_sem=agr.at[t, slot + h],
            device_id={"tensor": sib},
            device_id_type=MESH,
        ).wait_recv()

    def project(t, h, b, first=False):
        rows_f = xb[t, b, h * half : (h + 1) * half, :].astype(F32)
        square = rows_f * rows_f
        total = square[:, 0:HD]
        for g in range(1, C // HD):
            total = total + square[:, g * HD : (g + 1) * HD]
        gain = in_gain[:, pl.ds(pl.multiple_of(b * C, C), C)]
        product = jnp.dot((rows_f * gain).astype(BF16), wqkv[b], preferred_element_type=F32)
        if first:
            ss[h] = total
            acc[h] = product
        else:
            ss[h] += total
            acc[h] += product

    def start(t, h):
        @pl.when(s > 0)
        def _():
            arrived(t, h, 0, me)

        if h == 0:

            @pl.when(s == 0)
            def _():
                enter(t).wait()

        for k in range(4):
            gather(t, h, k).start()

    def forward(t, h, which):
        slot, b, k = ((4, left, 4), (6, right, 5), (12, opp, 6))[which]
        arrived(t, h, slot, b)
        gather(t, h, k).start()

    def appended(step):
        return pltpu.make_async_copy(
            kv.at[pl.ds(pl.multiple_of(off + step * R, R), R)],
            kv_out.at[pl.ds(step * R, R)],
            out_sem.at[step],
        )

    def attention(t, h):
        scale = lax.rsqrt(jnp.sum(ss[h], axis=-1, keepdims=True) * (1.0 / D) + EPS)
        cos = cs[t, h * half : (h + 1) * half, :]
        sin = sn[t, h * half : (h + 1) * half, :]

        def head(value, gain):
            value = value * scale
            mean = jnp.sum(value * value, axis=-1, keepdims=True) * (1.0 / HD)
            value = value * lax.rsqrt(mean + EPS) * gain
            return value * cos + pltpu.roll(value, HD // 2, 1) * sin

        for g in range(G):
            query = head(acc[h, :, g * HD : (g + 1) * HD], q_gain[...])
            qs[g * half : (g + 1) * half, :] = (query * (math.log2(math.e) * HD**-0.5)).astype(BF16)

        if h == 0:

            @pl.when(t == 0)
            def _():
                load(6).wait()

        here = pl.ds(pl.multiple_of(off + t * R + h * half, half), half)
        kv[here, 0:HD] = head(acc[h, :, HC : HC + HD], k_gain[...]).astype(BF16)
        kv[here, HD:] = (acc[h, :, HC + HD :] * scale).astype(BF16)
        if h == 1:
            appended(t).start()

        whole = (off + t * R) // chunk

        def block_of(at):
            return pl.ds(pl.multiple_of(at * chunk, chunk), chunk)

        def score(at):
            return jnp.exp2(
                lax.dot_general(
                    qs[...],
                    kv[block_of(at), 0:HD],
                    (((1,), (1,)), ((), ())),
                    preferred_element_type=F32,
                )
            )

        def weigh(at, place):
            values = jnp.concatenate([kv[block_of(at), HD:], jnp.ones((chunk, HD), BF16)], axis=1)
            pv[...] += jnp.dot(ps[place], values, preferred_element_type=F32)

        pv[...] = jnp.zeros_like(pv)
        slot = whole * chunk + lax.broadcasted_iota(jnp.int32, (half, chunk), 1)
        last = off + t * R + h * half + lax.broadcasted_iota(jnp.int32, (half, chunk), 0)
        weight = jnp.where((slot <= last)[None], score(whole).reshape(G, half, chunk), 0.0)
        ps[0] = weight.reshape(G * half, chunk).astype(BF16)

        def pair(i, carry):
            ps[1] = score(2 * i).astype(BF16)
            weigh(jnp.where(i == 0, whole, 2 * i - 1), 0)
            ps[0] = score(2 * i + 1).astype(BF16)
            weigh(2 * i, 1)
            return carry

        lax.fori_loop(0, whole // 2, pair, 0)
        left_over = jnp.where(whole < 2, whole, 2 * (whole // 2) - 1)

        @pl.when(whole % 2 == 1)
        def _():
            ps[1] = score(whole - 1).astype(BF16)
            weigh(left_over, 0)
            weigh(whole - 1, 1)

        @pl.when(whole % 2 == 0)
        def _():
            weigh(left_over, 0)

        for g in range(G):
            found = pv[g * half : (g + 1) * half, :]
            att[t, 0, h * half : (h + 1) * half, g * HD : (g + 1) * HD] = (
                found[:, 0:HD] / found[:, HD:]
            ).astype(BF16)
        reduce(t, h, 0).start()

    def reduce(t, h, k):
        these = pl.ds(h * half, half)
        if k == 0:
            source, target = att.at[t, 0, these], att.at[t, 1, these]
        else:
            source, target = nb_src.at[t, k - 1, these], nb_dst.at[t, k - 1, these]
        return pltpu.make_async_remote_copy(
            src_ref=source,
            dst_ref=target,
            send_sem=rss.at[t, 4 * h + k],
            recv_sem=rsr.at[t, 4 * h + k],
            device_id={"tensor": (sib, opp, right, left)[k]},
            device_id_type=MESH,
        )

    def part(t, h, b, heads, table):
        return jnp.dot(
            att[t, heads, h * half : (h + 1) * half, :], table[b], preferred_element_type=F32
        )

    def own_part(t, h):
        if h == 0:

            @pl.when(t == 0)
            def _():
                for j in range(ring):
                    load(7 + j).wait()
                    weights(j).wait_recv()

        for d, b in enumerate((opp, right, left, me)):
            keep[h, d] = part(t, h, b // 2, 0, wo)

    def other_part(t, h):
        these = slice(h * half, (h + 1) * half)
        reduce(t, h, 0).wait_recv()
        for d, b in enumerate((opp, right, left)):
            nb_src[t, d, these, :] = (keep[h, d] + part(t, h, b // 2, 1, wo_sib)).astype(BF16)
            reduce(t, h, 1 + d).start()
        keep[h, 3] += part(t, h, x, 1, wo_sib) + xb[t, me, these, :].astype(F32)

    def inject():
        pltpu.make_async_remote_copy(
            src_ref=fbuf.at[pl.ds(0, (S - 1) * PAD)],
            dst_ref=fbuf.at[pl.ds(0, (S - 1) * PAD)],
            send_sem=fs_sem.at[0],
            recv_sem=fr_sem,
            device_id={"section": 0},
            device_id_type=MESH,
        ).wait_recv()
        for step in range(steps):
            inj[step] = lax.dot_general(
                fbuf[:, C + step * R : C + (step + 1) * R],
                fbuf[:, 0:C],
                (((0,), (0,)), ((), ())),
                preferred_element_type=F32,
            )

    def finish(t, h):
        these = slice(h * half, (h + 1) * half)

        @pl.when(s < levels)
        def _():
            keep[h, 3] += inj[t, these, :]

        total = keep[h, 3]
        for d in (1, 2, 0):
            reduce(t, h, 1 + d).wait_recv()
            total = total + nb_dst[t, d, these, :].astype(F32)
        yb[t, these, :] = total.astype(BF16)

        @pl.when((t == 0) & (s < S - 1))
        def _():
            shift(yb.at[0], 1, h).start()

    def step_body(t, carry):
        @pl.when(t > 0)
        def _():
            finish(jnp.maximum(t - 1, 0), 1)

        @pl.when(t == 0)
        def _():
            for i in (4, 5):
                load(i).wait()

        project(t, 0, me, True)
        arrived(t, 0, 2, sib)
        project(t, 0, sib)
        forward(t, 0, 0)
        forward(t, 0, 1)
        project(t, 0, left)
        forward(t, 0, 2)
        project(t, 0, right)

        @pl.when(t > 0)
        def _():
            start(t, 1)

        project(t, 0, opp)
        arrived(t, 0, 8, sleft)
        project(t, 0, sleft)
        arrived(t, 0, 10, sright)
        project(t, 0, sright)
        arrived(t, 0, 14, sopp)
        project(t, 0, sopp)

        @pl.when(t == 0)
        def _():
            for which in range(3):
                forward(t, 1, which)

        attention(t, 0)
        own_part(t, 0)
        other_part(t, 0)

        @pl.when(t > 0)
        def _():
            for which in range(3):
                forward(t, 1, which)

        project(t, 1, me, True)
        project(t, 1, left)
        project(t, 1, right)
        project(t, 1, opp)
        for slot, b in ((2, sib), (8, sleft), (10, sright), (14, sopp)):
            arrived(t, 1, slot, b)
            project(t, 1, b)
        attention(t, 1)
        own_part(t, 1)

        @pl.when((t == 0) & (s < levels))
        def _():
            inject()

        finish(t, 0)
        other_part(t, 1)

        @pl.when(t + 1 < steps)
        def _():
            start(jnp.minimum(t + 1, steps - 1), 0)

        return carry

    start(0, 0)
    start(0, 1)
    for level in range(levels):

        @pl.when(s != level)
        def _():
            feature(level).start()

    lax.fori_loop(0, steps, step_body, 0)

    def sent(t, carry):
        for h in range(2):
            for k in range(7):
                gather(t, h, k).wait_send()
            for k in range(4):
                reduce(t, h, k).wait_send()
        return carry

    lax.fori_loop(0, steps - 1, sent, 0)

    @pl.when(s < S - 1)
    def _():
        for h in range(2):
            shift(pend, 0, h).wait_send()
            shift(yb.at[0], 1, h).wait_send()

    for j in range(ring):
        weights(j).wait_send()

    for level in range(levels):

        @pl.when(s != level)
        def _():
            feature(level).wait_send()

    finish(steps - 1, 1)
    final = pltpu.make_async_copy(yb.at[steps - 1], out, out_sem.at[steps])
    final.start()
    sent(steps - 1, 0)
    for step in range(steps):
        appended(step).wait()
    final.wait()


def deliver(hidden, appended, hidden_out, appended_out, held, kept, in_sem, out_sem):
    ways = [(hidden, held, hidden_out), (appended, kept, appended_out)]
    for i, (source, between, target) in enumerate(ways):
        pltpu.make_async_copy(source, between, in_sem.at[i]).start()
    for i, (source, between, target) in enumerate(ways):
        pltpu.make_async_copy(source, between, in_sem.at[i]).wait()
        pltpu.make_async_copy(between, target, out_sem.at[i]).start()
    for i, (source, between, target) in enumerate(ways):
        pltpu.make_async_copy(between, target, out_sem.at[i]).wait()


def body(sections, tensors, pend, emb, wq, wkv, wo, memo, in_gain, q_gain, k_gain, feat, pos):
    R, C = pend.shape
    steps = emb.shape[0] // R
    D = C * tensors
    HC = wq.shape[2]
    HD = 128
    rows, levels = feat.shape[0], feat.shape[1]
    cap = memo.shape[1]
    chunk = 8 * R
    slots = -(-(cap + steps * R) // chunk) * chunk
    anyspec = pl.BlockSpec(memory_space=pl.ANY)
    V = pltpu.VMEM
    DMA = pltpu.SemaphoreType.DMA
    hidden, appended = pl.pallas_call(
        functools.partial(kernel, sections),
        out_shape=(
            jax.ShapeDtypeStruct((R, C), BF16),
            jax.ShapeDtypeStruct((steps * R, 2 * HD), BF16),
        ),
        in_specs=[anyspec] * 10 + [pl.BlockSpec(memory_space=pltpu.SMEM)],
        out_specs=(anyspec, anyspec),
        scratch_shapes=[
            V((tensors, C, HC + 2 * HD), BF16),
            V((tensors // 2, HC, C), BF16),
            V((slots, 2 * HD), BF16),
            V((1, D), F32),
            V((1, HD), F32),
            V((1, HD), F32),
            V((rows, levels, C), BF16),
            V((levels, PAD, C + steps * R), BF16),
            V((sections * PAD, C + steps * R), BF16),
            V((steps, R, C), F32),
            V((steps, R, HD), F32),
            V((steps, R, HD), F32),
            V((steps, tensors, R, C), BF16),
            V((2, R // 2, HD), F32),
            V((2, R // 2, HC + 2 * HD), F32),
            V((HC // HD * R // 2, HD), BF16),
            V((2, HC // HD * R // 2, chunk), BF16),
            V((HC // HD * R // 2, 2 * HD), F32),
            V((steps, 2, R, HC), BF16),
            V((tensors // 2, HC, C), BF16),
            V((steps, 3, R, C), BF16),
            V((steps, 3, R, C), BF16),
            V((2, 4, R // 2, C), F32),
            V((steps, R, C), BF16),
            DMA((7 + tensors // 2,)),
            DMA((steps,)),
            DMA((levels,)),
            DMA,
            DMA((steps, 16)),
            DMA((steps, 16)),
            DMA((steps, 8)),
            DMA((steps, 8)),
            DMA((tensors // 2,)),
            DMA((tensors // 2,)),
            DMA((steps + 1,)),
        ],
        compiler_params=pltpu.CompilerParams(
            collective_id=0, has_side_effects=True, vmem_limit_bytes=64 * 1024 * 1024
        ),
    )(
        pend,
        emb,
        wq.reshape(tensors, C, HC),
        wkv.reshape(tensors, C, 2 * HD),
        wo.reshape(HC, D),
        memo.reshape(cap, 2 * HD),
        in_gain,
        q_gain,
        k_gain,
        feat,
        pos,
    )
    hidden, appended = pl.pallas_call(
        deliver,
        out_shape=(
            jax.ShapeDtypeStruct((R, C), BF16),
            jax.ShapeDtypeStruct((steps * R, 2 * HD), BF16),
        ),
        in_specs=[anyspec] * 2,
        out_specs=(anyspec, anyspec),
        scratch_shapes=[V((R, C), BF16), V((steps * R, 2 * HD), BF16), DMA((2,)), DMA((2,))],
        compiler_params=pltpu.CompilerParams(vmem_limit_bytes=64 * 1024 * 1024),
    )(hidden, appended)
    return hidden, appended.reshape(1, steps * R, 2 * HD)


def solution(mesh):
    return jax.shard_map(
        functools.partial(body, mesh.shape["section"], mesh.shape["tensor"]),
        mesh=mesh,
        in_specs=(
            P("section", "tensor"),
            P(None, "tensor"),
            P("section", None, "tensor"),
            P("section", None, "tensor"),
            P("section", "tensor", None),
            P("section", None, "tensor"),
            P("section", None),
            P("section", None),
            P("section", None),
            P("section", None, "tensor"),
            P("section"),
        ),
        out_specs=(P("section", "tensor"), P("section", None, "tensor")),
        check_vma=False,
    )
```

```python
import functools
import math

import jax
import jax.numpy as jnp
from jax import lax
from jax.experimental import pallas as pl
from jax.experimental.pallas import tpu as pltpu
from jax.sharding import PartitionSpec as P

MESH = pl.DeviceIdType.MESH
EPS = 1e-06
THETA = 5000000.0
PAD = 16
F32 = jnp.float32
BF16 = jnp.bfloat16


def kernel(
    sections,
    pend,
    emb,
    wq_h,
    wkv_h,
    wo_h,
    memo,
    in_gain_h,
    q_gain_h,
    k_gain_h,
    feat_h,
    pos,
    out,
    kv_out,
    pend_v,
    wqkv,
    wo,
    kv,
    in_gain,
    q_gain,
    k_gain,
    feat,
    msg,
    fbuf,
    inj,
    cs,
    sn,
    xb,
    ss,
    acc,
    qs,
    ps,
    pv,
    att,
    wo_sib,
    nb_src,
    nb_dst,
    keep,
    yb,
    load_sem,
    emb_sem,
    fs_sem,
    fr_sem,
    ags,
    agr,
    rss,
    rsr,
    ws,
    wr,
    out_sem,
):
    S = sections
    steps, T, R, C = xb.shape
    half = R // 2
    HD = 128
    HC = att.shape[3]
    G = HC // HD
    D = T * C
    rows, levels = feat.shape[0], feat.shape[1]
    chunk = 8 * R
    s = lax.axis_index("section")
    me = lax.axis_index("tensor")
    x = me // 2
    c = me % 2
    ring = T // 2

    def block(step, parity):
        return 2 * ((x + step) % ring) + parity

    sib = block(0, 1 - c)
    right, left, opp = block(1, c), block(ring - 1, c), block(2, c)
    sright, sleft, sopp = block(1, 1 - c), block(ring - 1, 1 - c), block(2, 1 - c)
    off = pl.multiple_of((S - 1 - s) * R, R)

    barrier = pltpu.get_barrier_semaphore()
    for peer in (sib, right, left, opp):
        pl.semaphore_signal(barrier, inc=1, device_id={"tensor": peer}, device_id_type=MESH)

    @pl.when(s < levels)
    def _():
        def greet(k, carry):
            @pl.when(k != s)
            def _():
                pl.semaphore_signal(barrier, inc=1, device_id={"section": k}, device_id_type=MESH)

            return carry

        lax.fori_loop(0, S, greet, 0)

    @pl.when(s >= levels)
    def _():
        pl.semaphore_signal(barrier, inc=1, device_id={"section": s - 1}, device_id_type=MESH)

    ends = [
        (pend, pend_v),
        (feat_h, feat),
        (in_gain_h, in_gain),
        (q_gain_h, q_gain),
        (k_gain_h, k_gain),
        (wq_h, wqkv.at[:, :, pl.ds(0, HC)]),
        (wkv_h, wqkv.at[:, :, pl.ds(HC, 2 * HD)]),
        (memo, kv.at[pl.ds(0, memo.shape[0])]),
    ] + [
        (wo_h.at[:, pl.ds(pl.multiple_of((2 * j + c) * C, C), C)], wo.at[j])
        for j in range(ring)
    ]

    def load(i):
        return pltpu.make_async_copy(*ends[i], load_sem.at[i])

    for i in range(8 + ring):
        load(i).start()

    def enter(step):
        return pltpu.make_async_copy(
            emb.at[pl.ds(step * R, R)], xb.at[step, me], emb_sem.at[step]
        )

    @pl.when(s == 0)
    def _():
        for step in range(steps):
            enter(step).start()

    peers = 4 + levels - jnp.where(s < levels, 1, 0)
    peers = peers + jnp.where((s >= levels - 1) & (s < S - 1), 1, 0)
    pl.semaphore_wait(barrier, peers)

    def shift(source, step, h):
        return pltpu.make_async_remote_copy(
            src_ref=source.at[pl.ds(h * half, half)],
            dst_ref=xb.at[step, me, pl.ds(h * half, half)],
            send_sem=ags.at[step, h],
            recv_sem=agr.at[step, h],
            device_id={"section": jnp.minimum(s + 1, S - 1)},
            device_id_type=MESH,
        )

    load(0).wait()

    @pl.when(s < S - 1)
    def _():
        for h in range(2):
            shift(pend_v, 0, h).start()

    def weights(j):
        return pltpu.make_async_remote_copy(
            src_ref=wo_h.at[:, pl.ds(pl.multiple_of((2 * j + 1 - c) * C, C), C)],
            dst_ref=wo_sib.at[j],
            send_sem=ws.at[j],
            recv_sem=wr.at[j],
            device_id={"tensor": sib},
            device_id_type=MESH,
        )

    for j in range(ring):
        weights(j).start()

    for i in range(1, 5):
        load(i).wait()
    col = lax.broadcasted_iota(jnp.int32, (PAD, steps * R), 1)
    row = lax.broadcasted_iota(jnp.int32, (PAD, steps * R), 0)
    place = jnp.full((PAD, steps * R), -1000000, jnp.int32)
    for r in range(rows):
        place = jnp.where(row == r, pos[r], place)
    msg[...] = jnp.zeros_like(msg)
    everything = feat[...].astype(F32)
    for level in range(levels):
        msg[level, 0:rows, 0:C] = everything[:, level, :].astype(BF16)
        hit = place - (levels - 1 - level) * R == col
        msg[level, :, C:] = jnp.where(hit, 1.0, 0.0).astype(BF16)

    def feature(level):
        return pltpu.make_async_remote_copy(
            src_ref=msg.at[level],
            dst_ref=fbuf.at[pl.ds(s * PAD, PAD)],
            send_sem=fs_sem.at[level],
            recv_sem=fr_sem,
            device_id={"section": level},
            device_id_type=MESH,
        )

    for level in range(levels):

        @pl.when(s == level)
        def _():
            fbuf[pl.ds(pl.multiple_of(s * PAD, PAD), PAD), :] = msg[level]

    lane = lax.broadcasted_iota(jnp.int32, (R, HD), 1)
    fold = jnp.where(lane < HD // 2, lane, lane - HD // 2).astype(F32)
    frequency = jnp.exp(fold * (-2.0 * math.log(THETA) / HD))
    for step in range(steps):
        place = off + step * R + lax.broadcasted_iota(jnp.int32, (R, HD), 0)
        angle = place.astype(F32) * frequency
        cs[step] = jnp.cos(angle)
        sn[step] = jnp.where(lane < HD // 2, -jnp.sin(angle), jnp.sin(angle))
    tail = kv.shape[0] - memo.shape[0]
    kv[pl.ds(memo.shape[0], tail), :] = jnp.zeros((tail, 2 * HD), BF16)

    def piece(t, b, h):
        return xb.at[t, b, pl.ds(h * half, half)]

    def gather(t, h, k):
        b, peer, slot = (
            (me, opp, 12),
            (me, right, 4),
            (me, left, 6),
            (me, sib, 2),
            (left, sib, 8),
            (right, sib, 10),
            (opp, sib, 14),
        )[k]
        return pltpu.make_async_remote_copy(
            src_ref=piece(t, b, h),
            dst_ref=piece(t, b, h),
            send_sem=ags.at[t, 2 + 7 * h + k],
            recv_sem=agr.at[t, slot + h],
            device_id={"tensor": peer},
            device_id_type=MESH,
        )

    def arrived(t, h, slot, b):
        pltpu.make_async_remote_copy(
            src_ref=piece(t, b, h),
            dst_ref=piece(t, b, h),
            send_sem=ags.at[t, 2],
            recv_sem=agr.at[t, slot + h],
            device_id={"tensor": sib},
            device_id_type=MESH,
        ).wait_recv()

    def project(t, halves, b, first=False):
        rows_f = xb[t, b, halves[0] * half : (halves[-1] + 1) * half, :].astype(F32)
        square = rows_f * rows_f
        total = square[:, 0:HD]
        for g in range(1, C // HD):
            total = total + square[:, g * HD : (g + 1) * HD]
        gain = in_gain[:, pl.ds(pl.multiple_of(b * C, C), C)]
        product = jnp.dot((rows_f * gain).astype(BF16), wqkv[b], preferred_element_type=F32)
        for i, h in enumerate(halves):
            these = slice(i * half, (i + 1) * half)
            if first:
                ss[h] = total[these]
                acc[h] = product[these]
            else:
                ss[h] += total[these]
                acc[h] += product[these]

    def start(t, h):
        @pl.when(s > 0)
        def _():
            arrived(t, h, 0, me)

        if h == 0:

            @pl.when(s == 0)
            def _():
                enter(t).wait()

        for k in range(4):
            gather(t, h, k).start()

    def forward(t, h, which):
        slot, b, k = ((4, left, 4), (6, right, 5), (12, opp, 6))[which]
        arrived(t, h, slot, b)
        gather(t, h, k).start()

    def appended(step):
        return pltpu.make_async_copy(
            kv.at[pl.ds(pl.multiple_of(off + step * R, R), R)],
            kv_out.at[pl.ds(step * R, R)],
            out_sem.at[step],
        )

    def heads(t, h):
        scale = lax.rsqrt(jnp.sum(ss[h], axis=-1, keepdims=True) * (1.0 / D) + EPS)
        cos = cs[t, h * half : (h + 1) * half, :]
        sin = sn[t, h * half : (h + 1) * half, :]

        def head(value, gain):
            value = value * scale
            mean = jnp.sum(value * value, axis=-1, keepdims=True) * (1.0 / HD)
            value = value * lax.rsqrt(mean + EPS) * gain
            return value * cos + pltpu.roll(value, HD // 2, 1) * sin

        for g in range(G):
            query = head(acc[h, :, g * HD : (g + 1) * HD], q_gain[...])
            qs[g * half : (g + 1) * half, :] = (query * (math.log2(math.e) * HD**-0.5)).astype(BF16)

        if h == 0 and t == 0:
            load(7).wait()

        here = pl.ds(pl.multiple_of(off + t * R + h * half, half), half)
        kv[here, 0:HD] = head(acc[h, :, HC : HC + HD], k_gain[...]).astype(BF16)
        kv[here, HD:] = (acc[h, :, HC + HD :] * scale).astype(BF16)
        if h == 1:
            appended(t).start()

    def attend(t, h):
        whole = (off + t * R) // chunk

        def block_of(at):
            return pl.ds(pl.multiple_of(at * chunk, chunk), chunk)

        def score(at):
            return jnp.exp2(
                lax.dot_general(
                    qs[...],
                    kv[block_of(at), 0:HD],
                    (((1,), (1,)), ((), ())),
                    preferred_element_type=F32,
                )
            )

        def weigh(at, place):
            values = jnp.concatenate([kv[block_of(at), HD:], jnp.ones((chunk, HD), BF16)], axis=1)
            pv[...] += jnp.dot(ps[place], values, preferred_element_type=F32)

        pv[...] = jnp.zeros_like(pv)
        slot = whole * chunk + lax.broadcasted_iota(jnp.int32, (half, chunk), 1)
        last = off + t * R + h * half + lax.broadcasted_iota(jnp.int32, (half, chunk), 0)
        weight = jnp.where((slot <= last)[None], score(whole).reshape(G, half, chunk), 0.0)
        ps[0] = weight.reshape(G * half, chunk).astype(BF16)

        def pair(i, carry):
            ps[1] = score(2 * i).astype(BF16)
            weigh(jnp.where(i == 0, whole, 2 * i - 1), 0)
            ps[0] = score(2 * i + 1).astype(BF16)
            weigh(2 * i, 1)
            return carry

        lax.fori_loop(0, whole // 2, pair, 0)
        left_over = jnp.where(whole < 2, whole, 2 * (whole // 2) - 1)

        @pl.when(whole % 2 == 1)
        def _():
            ps[1] = score(whole - 1).astype(BF16)
            weigh(left_over, 0)
            weigh(whole - 1, 1)

        @pl.when(whole % 2 == 0)
        def _():
            weigh(left_over, 0)

        for g in range(G):
            found = pv[g * half : (g + 1) * half, :]
            att[t, 0, h * half : (h + 1) * half, g * HD : (g + 1) * HD] = (
                found[:, 0:HD] / found[:, HD:]
            ).astype(BF16)
        reduce(t, h, 0).start()

    def reduce(t, h, k):
        these = pl.ds(h * half, half)
        if k == 0:
            source, target = att.at[t, 0, these], att.at[t, 1, these]
        else:
            source, target = nb_src.at[t, k - 1, these], nb_dst.at[t, k - 1, these]
        return pltpu.make_async_remote_copy(
            src_ref=source,
            dst_ref=target,
            send_sem=rss.at[t, 4 * h + k],
            recv_sem=rsr.at[t, 4 * h + k],
            device_id={"tensor": (sib, opp, right, left)[k]},
            device_id_type=MESH,
        )

    def part(t, h, b, heads, table):
        return jnp.dot(
            att[t, heads, h * half : (h + 1) * half, :], table[b], preferred_element_type=F32
        )

    def own_part(t, h):
        if h == 0 and t == 0:
            for j in range(ring):
                load(8 + j).wait()
                weights(j).wait_recv()

        for d, b in enumerate((opp, right, left, me)):
            keep[h, d] = part(t, h, b // 2, 0, wo)

    def other_part(t, h):
        these = slice(h * half, (h + 1) * half)
        reduce(t, h, 0).wait_recv()
        for d, b in enumerate((opp, right, left)):
            nb_src[t, d, these, :] = (keep[h, d] + part(t, h, b // 2, 1, wo_sib)).astype(BF16)
            reduce(t, h, 1 + d).start()
        keep[h, 3] += part(t, h, x, 1, wo_sib) + xb[t, me, these, :].astype(F32)

    def inject():
        pltpu.make_async_remote_copy(
            src_ref=fbuf.at[pl.ds(0, (S - 1) * PAD)],
            dst_ref=fbuf.at[pl.ds(0, (S - 1) * PAD)],
            send_sem=fs_sem.at[0],
            recv_sem=fr_sem,
            device_id={"section": 0},
            device_id_type=MESH,
        ).wait_recv()
        for step in range(steps):
            inj[step] = lax.dot_general(
                fbuf[:, C + step * R : C + (step + 1) * R],
                fbuf[:, 0:C],
                (((0,), (0,)), ((), ())),
                preferred_element_type=F32,
            )

    def finish(t, h):
        these = slice(h * half, (h + 1) * half)

        @pl.when(s < levels)
        def _():
            keep[h, 3] += inj[t, these, :]

        total = keep[h, 3]
        for d in (1, 2, 0):
            reduce(t, h, 1 + d).wait_recv()
            total = total + nb_dst[t, d, these, :].astype(F32)
        yb[t, these, :] = total.astype(BF16)

        if t + 1 < steps:

            @pl.when(s < S - 1)
            def _():
                shift(yb.at[t], t + 1, h).start()

    both = (0, 1)
    for h in both:
        start(0, h)
    for level in range(levels):

        @pl.when(s != level)
        def _():
            feature(level).start()

    for i in (5, 6):
        load(i).wait()
    project(0, both, me, True)
    for h in both:
        arrived(0, h, 2, sib)
    project(0, both, sib)
    for h in both:
        forward(0, h, 0)
        forward(0, h, 1)
    project(0, both, left)
    for h in both:
        forward(0, h, 2)
    project(0, both, right)
    project(0, both, opp)
    for slot, b in ((8, sleft), (10, sright), (14, sopp)):
        for h in both:
            arrived(0, h, slot, b)
        project(0, both, b)
    heads(0, 0)
    attend(0, 0)
    own_part(0, 0)
    heads(0, 1)
    other_part(0, 0)
    attend(0, 1)
    own_part(0, 1)

    @pl.when(s < levels)
    def _():
        inject()

    other_part(0, 1)
    finish(0, 0)

    for t in range(1, steps):
        start(t, 0)
        finish(t - 1, 1)
        project(t, (0,), me, True)
        arrived(t, 0, 2, sib)
        project(t, (0,), sib)
        start(t, 1)
        forward(t, 0, 0)
        forward(t, 0, 1)
        project(t, (0,), left)
        forward(t, 0, 2)
        project(t, (0,), right)
        project(t, (0,), opp)
        for slot, b in ((8, sleft), (10, sright), (14, sopp)):
            arrived(t, 0, slot, b)
            project(t, (0,), b)
        heads(t, 0)
        attend(t, 0)
        for which in range(3):
            forward(t, 1, which)
        own_part(t, 0)
        project(t, (1,), me, True)
        project(t, (1,), left)
        other_part(t, 0)
        project(t, (1,), right)
        project(t, (1,), opp)
        for slot, b in ((2, sib), (8, sleft), (10, sright), (14, sopp)):
            arrived(t, 1, slot, b)
            project(t, (1,), b)
        heads(t, 1)
        attend(t, 1)
        own_part(t, 1)
        other_part(t, 1)
        finish(t, 0)

    def sent(t, carry):
        for h in range(2):
            for k in range(7):
                gather(t, h, k).wait_send()
            for k in range(4):
                reduce(t, h, k).wait_send()
        return carry

    lax.fori_loop(0, steps - 1, sent, 0)

    @pl.when(s < S - 1)
    def _():
        for h in range(2):
            shift(pend_v, 0, h).wait_send()
            shift(yb.at[0], 1, h).wait_send()

    for j in range(ring):
        weights(j).wait_send()

    for level in range(levels):

        @pl.when(s != level)
        def _():
            feature(level).wait_send()

    def final(h):
        these = pl.ds(h * half, half)
        return pltpu.make_async_copy(
            yb.at[steps - 1, these], out.at[these], out_sem.at[steps + h]
        )

    final(0).start()
    sent(steps - 1, 0)
    for step in range(steps):
        appended(step).wait()
    finish(steps - 1, 1)
    final(1).start()
    for h in both:
        final(h).wait()


def deliver(hidden, appended, hidden_out, appended_out, held, kept, in_sem, out_sem):
    ways = [(hidden, held, hidden_out), (appended, kept, appended_out)]
    for i, (source, between, target) in enumerate(ways):
        pltpu.make_async_copy(source, between, in_sem.at[i]).start()
    for i, (source, between, target) in enumerate(ways):
        pltpu.make_async_copy(source, between, in_sem.at[i]).wait()
        pltpu.make_async_copy(between, target, out_sem.at[i]).start()
    for i, (source, between, target) in enumerate(ways):
        pltpu.make_async_copy(between, target, out_sem.at[i]).wait()


def body(sections, tensors, pend, emb, wq, wkv, wo, memo, in_gain, q_gain, k_gain, feat, pos):
    R, C = pend.shape
    steps = emb.shape[0] // R
    D = C * tensors
    HC = wq.shape[2]
    HD = 128
    rows, levels = feat.shape[0], feat.shape[1]
    cap = memo.shape[1]
    chunk = 8 * R
    slots = -(-(cap + steps * R) // chunk) * chunk
    anyspec = pl.BlockSpec(memory_space=pl.ANY)
    V = pltpu.VMEM
    DMA = pltpu.SemaphoreType.DMA
    hidden, appended = pl.pallas_call(
        functools.partial(kernel, sections),
        out_shape=(
            jax.ShapeDtypeStruct((R, C), BF16),
            jax.ShapeDtypeStruct((steps * R, 2 * HD), BF16),
        ),
        in_specs=[anyspec] * 10 + [pl.BlockSpec(memory_space=pltpu.SMEM)],
        out_specs=(anyspec, anyspec),
        scratch_shapes=[
            V((R, C), BF16),
            V((tensors, C, HC + 2 * HD), BF16),
            V((tensors // 2, HC, C), BF16),
            V((slots, 2 * HD), BF16),
            V((1, D), F32),
            V((1, HD), F32),
            V((1, HD), F32),
            V((rows, levels, C), BF16),
            V((levels, PAD, C + steps * R), BF16),
            V((sections * PAD, C + steps * R), BF16),
            V((steps, R, C), F32),
            V((steps, R, HD), F32),
            V((steps, R, HD), F32),
            V((steps, tensors, R, C), BF16),
            V((2, R // 2, HD), F32),
            V((2, R // 2, HC + 2 * HD), F32),
            V((HC // HD * R // 2, HD), BF16),
            V((2, HC // HD * R // 2, chunk), BF16),
            V((HC // HD * R // 2, 2 * HD), F32),
            V((steps, 2, R, HC), BF16),
            V((tensors // 2, HC, C), BF16),
            V((steps, 3, R, C), BF16),
            V((steps, 3, R, C), BF16),
            V((2, 4, R // 2, C), F32),
            V((steps, R, C), BF16),
            DMA((8 + tensors // 2,)),
            DMA((steps,)),
            DMA((levels,)),
            DMA,
            DMA((steps, 16)),
            DMA((steps, 16)),
            DMA((steps, 8)),
            DMA((steps, 8)),
            DMA((tensors // 2,)),
            DMA((tensors // 2,)),
            DMA((steps + 2,)),
        ],
        compiler_params=pltpu.CompilerParams(
            collective_id=0, has_side_effects=True, vmem_limit_bytes=64 * 1024 * 1024
        ),
    )(
        pend,
        emb,
        wq.reshape(tensors, C, HC),
        wkv.reshape(tensors, C, 2 * HD),
        wo.reshape(HC, D),
        memo.reshape(cap, 2 * HD),
        in_gain,
        q_gain,
        k_gain,
        feat,
        pos,
    )
    hidden, appended = pl.pallas_call(
        deliver,
        out_shape=(
            jax.ShapeDtypeStruct((R, C), BF16),
            jax.ShapeDtypeStruct((steps * R, 2 * HD), BF16),
        ),
        in_specs=[anyspec] * 2,
        out_specs=(anyspec, anyspec),
        scratch_shapes=[V((R, C), BF16), V((steps * R, 2 * HD), BF16), DMA((2,)), DMA((2,))],
        compiler_params=pltpu.CompilerParams(vmem_limit_bytes=64 * 1024 * 1024),
    )(hidden, appended)
    return hidden, appended.reshape(1, steps * R, 2 * HD)


def solution(mesh):
    return jax.shard_map(
        functools.partial(body, mesh.shape["section"], mesh.shape["tensor"]),
        mesh=mesh,
        in_specs=(
            P("section", "tensor"),
            P(None, "tensor"),
            P("section", None, "tensor"),
            P("section", None, "tensor"),
            P("section", "tensor", None),
            P("section", None, "tensor"),
            P("section", None),
            P("section", None),
            P("section", None),
            P("section", None, "tensor"),
            P("section"),
        ),
        out_specs=(P("section", "tensor"), P("section", None, "tensor")),
        check_vma=False,
    )
```

```python
import functools
import math

import jax
import jax.numpy as jnp
from jax import lax
from jax.experimental import pallas as pl
from jax.experimental.pallas import tpu as pltpu
from jax.sharding import PartitionSpec as P

MESH = pl.DeviceIdType.MESH
EPS = 1e-06
THETA = 5000000.0
PAD = 16
F32 = jnp.float32
BF16 = jnp.bfloat16


def kernel(
    sections,
    pend,
    emb,
    wq_h,
    wkv_h,
    wo_h,
    memo,
    in_gain_h,
    q_gain_h,
    k_gain_h,
    feat_h,
    pos,
    out,
    kv_out,
    pend_v,
    wqkv,
    wo,
    kv,
    in_gain,
    q_gain,
    k_gain,
    feat,
    msg,
    fbuf,
    inj,
    cs,
    sn,
    xb,
    ss,
    acc,
    qs,
    ps,
    pv,
    att,
    wo_sib,
    nb_src,
    nb_dst,
    keep,
    yb,
    load_sem,
    emb_sem,
    fs_sem,
    fr_sem,
    ags,
    agr,
    rss,
    rsr,
    ws,
    wr,
    out_sem,
):
    S = sections
    steps, T, R, C = xb.shape
    half = R // 2
    HD = 128
    HC = att.shape[3]
    G = HC // HD
    D = T * C
    rows, levels = feat.shape[0], feat.shape[1]
    chunk = 8 * R
    s = lax.axis_index("section")
    me = lax.axis_index("tensor")
    x = me // 2
    c = me % 2
    ring = T // 2

    def block(step, parity):
        return 2 * ((x + step) % ring) + parity

    sib = block(0, 1 - c)
    right, left, opp = block(1, c), block(ring - 1, c), block(2, c)
    sright, sleft, sopp = block(1, 1 - c), block(ring - 1, 1 - c), block(2, 1 - c)
    off = pl.multiple_of((S - 1 - s) * R, R)

    barrier = pltpu.get_barrier_semaphore()
    for peer in (sib, right, left, opp):
        pl.semaphore_signal(barrier, inc=1, device_id={"tensor": peer}, device_id_type=MESH)

    @pl.when(s < levels)
    def _():
        def greet(k, carry):
            @pl.when(k != s)
            def _():
                pl.semaphore_signal(barrier, inc=1, device_id={"section": k}, device_id_type=MESH)

            return carry

        lax.fori_loop(0, S, greet, 0)

    @pl.when(s >= levels)
    def _():
        pl.semaphore_signal(barrier, inc=1, device_id={"section": s - 1}, device_id_type=MESH)

    ends = [
        (pend, pend_v),
        (feat_h, feat),
        (in_gain_h, in_gain),
        (q_gain_h, q_gain),
        (k_gain_h, k_gain),
        (wq_h, wqkv.at[:, :, pl.ds(0, HC)]),
        (wkv_h, wqkv.at[:, :, pl.ds(HC, 2 * HD)]),
        (memo, kv.at[pl.ds(0, memo.shape[0])]),
    ] + [
        (wo_h.at[:, pl.ds(pl.multiple_of((2 * j + c) * C, C), C)], wo.at[j])
        for j in range(ring)
    ]

    def load(i):
        return pltpu.make_async_copy(*ends[i], load_sem.at[i])

    for i in range(8 + ring):
        load(i).start()

    def enter(step):
        return pltpu.make_async_copy(
            emb.at[pl.ds(step * R, R)], xb.at[step, me], emb_sem.at[step]
        )

    @pl.when(s == 0)
    def _():
        for step in range(steps):
            enter(step).start()

    peers = 4 + levels - jnp.where(s < levels, 1, 0)
    peers = peers + jnp.where((s >= levels - 1) & (s < S - 1), 1, 0)
    pl.semaphore_wait(barrier, peers)

    def shift(source, step, h):
        return pltpu.make_async_remote_copy(
            src_ref=source.at[pl.ds(h * half, half)],
            dst_ref=xb.at[step, me, pl.ds(h * half, half)],
            send_sem=ags.at[step, h],
            recv_sem=agr.at[step, h],
            device_id={"section": jnp.minimum(s + 1, S - 1)},
            device_id_type=MESH,
        )

    load(0).wait()

    @pl.when(s < S - 1)
    def _():
        for h in range(2):
            shift(pend_v, 0, h).start()

    def weights(j):
        return pltpu.make_async_remote_copy(
            src_ref=wo_h.at[:, pl.ds(pl.multiple_of((2 * j + 1 - c) * C, C), C)],
            dst_ref=wo_sib.at[j],
            send_sem=ws.at[j],
            recv_sem=wr.at[j],
            device_id={"tensor": sib},
            device_id_type=MESH,
        )

    for j in range(ring):
        weights(j).start()

    for i in range(1, 5):
        load(i).wait()
    col = lax.broadcasted_iota(jnp.int32, (PAD, steps * R), 1)
    row = lax.broadcasted_iota(jnp.int32, (PAD, steps * R), 0)
    place = jnp.full((PAD, steps * R), -1000000, jnp.int32)
    for r in range(rows):
        place = jnp.where(row == r, pos[r], place)
    msg[...] = jnp.zeros_like(msg)
    everything = feat[...].astype(F32)
    for level in range(levels):
        msg[level, 0:rows, 0:C] = everything[:, level, :].astype(BF16)
        hit = place - (levels - 1 - level) * R == col
        msg[level, :, C:] = jnp.where(hit, 1.0, 0.0).astype(BF16)

    def feature(level):
        return pltpu.make_async_remote_copy(
            src_ref=msg.at[level],
            dst_ref=fbuf.at[pl.ds(s * PAD, PAD)],
            send_sem=fs_sem.at[level],
            recv_sem=fr_sem,
            device_id={"section": level},
            device_id_type=MESH,
        )

    for level in range(levels):

        @pl.when(s == level)
        def _():
            fbuf[pl.ds(pl.multiple_of(s * PAD, PAD), PAD), :] = msg[level]

    lane = lax.broadcasted_iota(jnp.int32, (R, HD), 1)
    fold = jnp.where(lane < HD // 2, lane, lane - HD // 2).astype(F32)
    frequency = jnp.exp(fold * (-2.0 * math.log(THETA) / HD))
    for step in range(steps):
        place = off + step * R + lax.broadcasted_iota(jnp.int32, (R, HD), 0)
        angle = place.astype(F32) * frequency
        cs[step] = jnp.cos(angle)
        sn[step] = jnp.where(lane < HD // 2, -jnp.sin(angle), jnp.sin(angle))
    tail = kv.shape[0] - memo.shape[0]
    kv[pl.ds(memo.shape[0], tail), :] = jnp.zeros((tail, 2 * HD), BF16)

    def piece(t, b, h):
        return xb.at[t, b, pl.ds(h * half, half)]

    def gather(t, h, k):
        b, peer, slot = (
            (me, opp, 12),
            (me, right, 4),
            (me, left, 6),
            (me, sib, 2),
            (left, sib, 8),
            (right, sib, 10),
            (opp, sib, 14),
        )[k]
        return pltpu.make_async_remote_copy(
            src_ref=piece(t, b, h),
            dst_ref=piece(t, b, h),
            send_sem=ags.at[t, 2 + 7 * h + k],
            recv_sem=agr.at[t, slot + h],
            device_id={"tensor": peer},
            device_id_type=MESH,
        )

    def arrived(t, h, slot, b):
        pltpu.make_async_remote_copy(
            src_ref=piece(t, b, h),
            dst_ref=piece(t, b, h),
            send_sem=ags.at[t, 2],
            recv_sem=agr.at[t, slot + h],
            device_id={"tensor": sib},
            device_id_type=MESH,
        ).wait_recv()

    def project(t, halves, b, first=False):
        rows_f = xb[t, b, halves[0] * half : (halves[-1] + 1) * half, :].astype(F32)
        square = rows_f * rows_f
        total = square[:, 0:HD]
        for g in range(1, C // HD):
            total = total + square[:, g * HD : (g + 1) * HD]
        gain = in_gain[:, pl.ds(pl.multiple_of(b * C, C), C)]
        product = jnp.dot((rows_f * gain).astype(BF16), wqkv[b], preferred_element_type=F32)
        for i, h in enumerate(halves):
            these = slice(i * half, (i + 1) * half)
            if first:
                ss[h] = total[these]
                acc[h] = product[these]
            else:
                ss[h] += total[these]
                acc[h] += product[these]

    def start(t, h):
        @pl.when(s > 0)
        def _():
            arrived(t, h, 0, me)

        if h == 0:

            @pl.when(s == 0)
            def _():
                enter(t).wait()

        for k in range(4):
            gather(t, h, k).start()

    def forward(t, h, which):
        slot, b, k = ((4, left, 4), (6, right, 5), (12, opp, 6))[which]
        arrived(t, h, slot, b)
        gather(t, h, k).start()

    def appended(step):
        return pltpu.make_async_copy(
            kv.at[pl.ds(pl.multiple_of(off + step * R, R), R)],
            kv_out.at[pl.ds(step * R, R)],
            out_sem.at[step],
        )

    def heads(t, h):
        scale = lax.rsqrt(jnp.sum(ss[h], axis=-1, keepdims=True) * (1.0 / D) + EPS)
        cos = cs[t, h * half : (h + 1) * half, :]
        sin = sn[t, h * half : (h + 1) * half, :]

        def head(value, gain):
            value = value * scale
            mean = jnp.sum(value * value, axis=-1, keepdims=True) * (1.0 / HD)
            value = value * lax.rsqrt(mean + EPS) * gain
            return value * cos + pltpu.roll(value, HD // 2, 1) * sin

        for g in range(G):
            query = head(acc[h, :, g * HD : (g + 1) * HD], q_gain[...])
            qs[g * half : (g + 1) * half, :] = (query * (math.log2(math.e) * HD**-0.5)).astype(BF16)

        if h == 0 and t == 0:
            load(7).wait()

        here = pl.ds(pl.multiple_of(off + t * R + h * half, half), half)
        kv[here, 0:HD] = head(acc[h, :, HC : HC + HD], k_gain[...]).astype(BF16)
        kv[here, HD:] = (acc[h, :, HC + HD :] * scale).astype(BF16)
        if h == 1:
            appended(t).start()

    def attend(t, h):
        whole = (off + t * R) // chunk

        def block_of(at):
            return pl.ds(pl.multiple_of(at * chunk, chunk), chunk)

        def score(at):
            return jnp.exp2(
                lax.dot_general(
                    qs[...],
                    kv[block_of(at), 0:HD],
                    (((1,), (1,)), ((), ())),
                    preferred_element_type=F32,
                )
            )

        def weigh(at, place):
            values = jnp.concatenate([kv[block_of(at), HD:], jnp.ones((chunk, HD), BF16)], axis=1)
            pv[...] += jnp.dot(ps[place], values, preferred_element_type=F32)

        pv[...] = jnp.zeros_like(pv)
        def masked(width):
            base = pl.multiple_of(whole * chunk, chunk)
            value = jnp.exp2(
                lax.dot_general(
                    qs[...],
                    kv[pl.ds(base, width), 0:HD],
                    (((1,), (1,)), ((), ())),
                    preferred_element_type=F32,
                )
            )
            slot = base + lax.broadcasted_iota(jnp.int32, (half, width), 1)
            last = off + t * R + h * half + lax.broadcasted_iota(jnp.int32, (half, width), 0)
            weight = jnp.where((slot <= last)[None], value.reshape(G, half, width), 0.0)
            ps[0, :, 0:width] = weight.reshape(G * half, width).astype(BF16)

        few = (off + t * R) % chunk <= R

        @pl.when(few)
        def _():
            masked(2 * R)
            ps[0, :, 2 * R :] = jnp.zeros((G * half, chunk - 2 * R), BF16)

        @pl.when(jnp.logical_not(few))
        def _():
            masked(chunk)

        def pair(i, carry):
            ps[1] = score(2 * i).astype(BF16)
            weigh(jnp.where(i == 0, whole, 2 * i - 1), 0)
            ps[0] = score(2 * i + 1).astype(BF16)
            weigh(2 * i, 1)
            return carry

        lax.fori_loop(0, whole // 2, pair, 0)
        left_over = jnp.where(whole < 2, whole, 2 * (whole // 2) - 1)

        @pl.when(whole % 2 == 1)
        def _():
            ps[1] = score(whole - 1).astype(BF16)
            weigh(left_over, 0)
            weigh(whole - 1, 1)

        @pl.when(whole % 2 == 0)
        def _():
            weigh(left_over, 0)

        for g in range(G):
            found = pv[g * half : (g + 1) * half, :]
            att[t, 0, h * half : (h + 1) * half, g * HD : (g + 1) * HD] = (
                found[:, 0:HD] / found[:, HD:]
            ).astype(BF16)
        reduce(t, h, 0).start()

    def reduce(t, h, k):
        these = pl.ds(h * half, half)
        if k == 0:
            source, target = att.at[t, 0, these], att.at[t, 1, these]
        else:
            source, target = nb_src.at[t, k - 1, these], nb_dst.at[t, k - 1, these]
        return pltpu.make_async_remote_copy(
            src_ref=source,
            dst_ref=target,
            send_sem=rss.at[t, 4 * h + k],
            recv_sem=rsr.at[t, 4 * h + k],
            device_id={"tensor": (sib, opp, right, left)[k]},
            device_id_type=MESH,
        )

    def part(t, h, b, heads, table):
        return jnp.dot(
            att[t, heads, h * half : (h + 1) * half, :], table[b], preferred_element_type=F32
        )

    def own_part(t, h):
        if h == 0 and t == 0:
            for j in range(ring):
                load(8 + j).wait()
                weights(j).wait_recv()

        for d, b in enumerate((opp, right, left, me)):
            keep[h, d] = part(t, h, b // 2, 0, wo)

    def other_part(t, h):
        these = slice(h * half, (h + 1) * half)
        reduce(t, h, 0).wait_recv()
        for d, b in enumerate((opp, right, left)):
            nb_src[t, d, these, :] = (keep[h, d] + part(t, h, b // 2, 1, wo_sib)).astype(BF16)
            reduce(t, h, 1 + d).start()
        keep[h, 3] += part(t, h, x, 1, wo_sib) + xb[t, me, these, :].astype(F32)

    def inject():
        pltpu.make_async_remote_copy(
            src_ref=fbuf.at[pl.ds(0, (S - 1) * PAD)],
            dst_ref=fbuf.at[pl.ds(0, (S - 1) * PAD)],
            send_sem=fs_sem.at[0],
            recv_sem=fr_sem,
            device_id={"section": 0},
            device_id_type=MESH,
        ).wait_recv()
        for step in range(steps):
            inj[step] = lax.dot_general(
                fbuf[:, C + step * R : C + (step + 1) * R],
                fbuf[:, 0:C],
                (((0,), (0,)), ((), ())),
                preferred_element_type=F32,
            )

    def finish(t, h):
        these = slice(h * half, (h + 1) * half)

        @pl.when(s < levels)
        def _():
            keep[h, 3] += inj[t, these, :]

        total = keep[h, 3]
        for d in (1, 2, 0):
            reduce(t, h, 1 + d).wait_recv()
            total = total + nb_dst[t, d, these, :].astype(F32)
        yb[t, these, :] = total.astype(BF16)

        if t + 1 < steps:

            @pl.when(s < S - 1)
            def _():
                shift(yb.at[t], t + 1, h).start()

    both = (0, 1)
    for h in both:
        start(0, h)
    for level in range(levels):

        @pl.when(s != level)
        def _():
            feature(level).start()

    for i in (5, 6):
        load(i).wait()
    project(0, both, me, True)
    for h in both:
        arrived(0, h, 2, sib)
    project(0, both, sib)
    for h in both:
        forward(0, h, 0)
        forward(0, h, 1)
    project(0, both, left)
    for h in both:
        forward(0, h, 2)
    project(0, both, right)
    project(0, both, opp)
    for slot, b in ((8, sleft), (10, sright), (14, sopp)):
        for h in both:
            arrived(0, h, slot, b)
        project(0, both, b)
    heads(0, 0)
    attend(0, 0)
    own_part(0, 0)
    heads(0, 1)
    other_part(0, 0)
    attend(0, 1)
    own_part(0, 1)

    @pl.when(s < levels)
    def _():
        inject()

    other_part(0, 1)
    finish(0, 0)

    for t in range(1, steps):
        start(t, 0)
        finish(t - 1, 1)
        project(t, (0,), me, True)
        arrived(t, 0, 2, sib)
        project(t, (0,), sib)
        start(t, 1)
        forward(t, 0, 0)
        forward(t, 0, 1)
        project(t, (0,), left)
        forward(t, 0, 2)
        project(t, (0,), right)
        project(t, (0,), opp)
        for slot, b in ((8, sleft), (10, sright), (14, sopp)):
            arrived(t, 0, slot, b)
            project(t, (0,), b)
        heads(t, 0)
        attend(t, 0)
        for which in range(3):
            forward(t, 1, which)
        own_part(t, 0)
        project(t, (1,), me, True)
        project(t, (1,), left)
        other_part(t, 0)
        project(t, (1,), right)
        project(t, (1,), opp)
        for slot, b in ((2, sib), (8, sleft), (10, sright), (14, sopp)):
            arrived(t, 1, slot, b)
            project(t, (1,), b)
        heads(t, 1)
        attend(t, 1)
        own_part(t, 1)
        other_part(t, 1)
        finish(t, 0)

    def sent(t, carry):
        for h in range(2):
            for k in range(7):
                gather(t, h, k).wait_send()
            for k in range(4):
                reduce(t, h, k).wait_send()
        return carry

    lax.fori_loop(0, steps - 1, sent, 0)

    @pl.when(s < S - 1)
    def _():
        for h in range(2):
            shift(pend_v, 0, h).wait_send()
            shift(yb.at[0], 1, h).wait_send()

    for j in range(ring):
        weights(j).wait_send()

    for level in range(levels):

        @pl.when(s != level)
        def _():
            feature(level).wait_send()

    def final(h):
        these = pl.ds(h * half, half)
        return pltpu.make_async_copy(
            yb.at[steps - 1, these], out.at[these], out_sem.at[steps + h]
        )

    final(0).start()
    sent(steps - 1, 0)
    for step in range(steps):
        appended(step).wait()
    finish(steps - 1, 1)
    final(1).start()
    for h in both:
        final(h).wait()


def deliver(hidden, appended, hidden_out, appended_out, held, kept, in_sem, out_sem):
    ways = [(hidden, held, hidden_out), (appended, kept, appended_out)]
    for i, (source, between, target) in enumerate(ways):
        pltpu.make_async_copy(source, between, in_sem.at[i]).start()
    for i, (source, between, target) in enumerate(ways):
        pltpu.make_async_copy(source, between, in_sem.at[i]).wait()
        pltpu.make_async_copy(between, target, out_sem.at[i]).start()
    for i, (source, between, target) in enumerate(ways):
        pltpu.make_async_copy(between, target, out_sem.at[i]).wait()


def body(sections, tensors, pend, emb, wq, wkv, wo, memo, in_gain, q_gain, k_gain, feat, pos):
    R, C = pend.shape
    steps = emb.shape[0] // R
    D = C * tensors
    HC = wq.shape[2]
    HD = 128
    rows, levels = feat.shape[0], feat.shape[1]
    cap = memo.shape[1]
    chunk = 8 * R
    slots = -(-(cap + steps * R) // chunk) * chunk
    anyspec = pl.BlockSpec(memory_space=pl.ANY)
    V = pltpu.VMEM
    DMA = pltpu.SemaphoreType.DMA
    hidden, appended = pl.pallas_call(
        functools.partial(kernel, sections),
        out_shape=(
            jax.ShapeDtypeStruct((R, C), BF16),
            jax.ShapeDtypeStruct((steps * R, 2 * HD), BF16),
        ),
        in_specs=[anyspec] * 10 + [pl.BlockSpec(memory_space=pltpu.SMEM)],
        out_specs=(anyspec, anyspec),
        scratch_shapes=[
            V((R, C), BF16),
            V((tensors, C, HC + 2 * HD), BF16),
            V((tensors // 2, HC, C), BF16),
            V((slots, 2 * HD), BF16),
            V((1, D), F32),
            V((1, HD), F32),
            V((1, HD), F32),
            V((rows, levels, C), BF16),
            V((levels, PAD, C + steps * R), BF16),
            V((sections * PAD, C + steps * R), BF16),
            V((steps, R, C), F32),
            V((steps, R, HD), F32),
            V((steps, R, HD), F32),
            V((steps, tensors, R, C), BF16),
            V((2, R // 2, HD), F32),
            V((2, R // 2, HC + 2 * HD), F32),
            V((HC // HD * R // 2, HD), BF16),
            V((2, HC // HD * R // 2, chunk), BF16),
            V((HC // HD * R // 2, 2 * HD), F32),
            V((steps, 2, R, HC), BF16),
            V((tensors // 2, HC, C), BF16),
            V((steps, 3, R, C), BF16),
            V((steps, 3, R, C), BF16),
            V((2, 4, R // 2, C), F32),
            V((steps, R, C), BF16),
            DMA((8 + tensors // 2,)),
            DMA((steps,)),
            DMA((levels,)),
            DMA,
            DMA((steps, 16)),
            DMA((steps, 16)),
            DMA((steps, 8)),
            DMA((steps, 8)),
            DMA((tensors // 2,)),
            DMA((tensors // 2,)),
            DMA((steps + 2,)),
        ],
        compiler_params=pltpu.CompilerParams(
            collective_id=0, has_side_effects=True, vmem_limit_bytes=64 * 1024 * 1024
        ),
    )(
        pend,
        emb,
        wq.reshape(tensors, C, HC),
        wkv.reshape(tensors, C, 2 * HD),
        wo.reshape(HC, D),
        memo.reshape(cap, 2 * HD),
        in_gain,
        q_gain,
        k_gain,
        feat,
        pos,
    )
    hidden, appended = pl.pallas_call(
        deliver,
        out_shape=(
            jax.ShapeDtypeStruct((R, C), BF16),
            jax.ShapeDtypeStruct((steps * R, 2 * HD), BF16),
        ),
        in_specs=[anyspec] * 2,
        out_specs=(anyspec, anyspec),
        scratch_shapes=[V((R, C), BF16), V((steps * R, 2 * HD), BF16), DMA((2,)), DMA((2,))],
        compiler_params=pltpu.CompilerParams(vmem_limit_bytes=64 * 1024 * 1024),
    )(hidden, appended)
    return hidden, appended.reshape(1, steps * R, 2 * HD)


def solution(mesh):
    return jax.shard_map(
        functools.partial(body, mesh.shape["section"], mesh.shape["tensor"]),
        mesh=mesh,
        in_specs=(
            P("section", "tensor"),
            P(None, "tensor"),
            P("section", None, "tensor"),
            P("section", None, "tensor"),
            P("section", "tensor", None),
            P("section", None, "tensor"),
            P("section", None),
            P("section", None),
            P("section", None),
            P("section", None, "tensor"),
            P("section"),
        ),
        out_specs=(P("section", "tensor"), P("section", None, "tensor")),
        check_vma=False,
    )
```
